32 devices in a mesh: seg: 2 (over y), row: 4 (over z), col: 4 (over x, core).
Axes of the slice: x: 2, y: 2, z: 4, core: 2. Of those that a mesh axis runs over, the one named last changes fastest.
Arguments:
- ld_tiles: bfloat16 [40, 40, 256, 256], P(('seg', 'row'), 'col'), parts along dimension 0, may hold values from -0.03125 to 0.03125
- tile_lists: int32 [40, 40], P(('seg', 'row'), 'col'), parts along dimension 0, may hold values from 0 to 19, as said below
- live_counts: int32 [40], P(('seg', 'row')), parts along dimension 0, may hold values from 10 to 40, as said below
- typed_mask: int32 [10240], P(('seg', 'row')), parts along dimension 0, may hold values 0 or 1
- solution: float32 [512, 5120], P(('seg', 'col'), 'row'), parts along dimension 0, may hold values from -6 to 6
- residual: float32 [512, 5120], P(('seg', 'col'), 'row'), parts along dimension 0
- direction: float32 [512, 5120], P(('seg', 'col'), 'row'), parts along dimension 0, may hold values from -6 to 6
Outputs:
- solution_next: float32 [512, 5120], P(('seg', 'col'), 'row'), parts along dimension 0
- residual_next: float32 [512, 5120], P(('seg', 'col'), 'row'), parts along dimension 0
- direction_next: float32 [512, 5120], P(('seg', 'col'), 'row'), parts along dimension 0
- imputed: float32 [512, 5120], P(('seg', 'col'), 'row'), parts along dimension 0
The draws below stay inside these ranges and needn't reach their ends.
There are 2 independent parts, one for each index of `seg`. The reference program is written for one: setup_inputs(seed, part) draws one part's arguments, and reference() takes and returns one part's arrays. A program takes and returns all parts, laid end to end along the dimension named above; each array names one. Nothing has to cross between parts.
Inputs may be any that keep to these rules, and one draw needn't show every extreme that they name: `tile_lists`: slot s of tile row t names t + o - 20 clipped to 0 .. 19, where the offsets o of a row are a permutation of 0 .. 39. `live_counts`: some tile row has all 40 slots live and another has 10.
All inputs are finite; a program needn't handle non-finite values. No bound on the sum of `typed_mask` on one device may be relied on, other than what follows from the above.
Results may differ from the reference program's by a relative error of at most 0.0029.
Values may be sent and summed in bfloat16 or wider, within the bound.
No kernel may reach another device: no remote copies, remote signals or barrier semaphores. Data moves between devices by JAX's collectives and lax.ppermute only.
A program may use at most 64 MiB of HBM per device.

```python
import math
import jax
import jax.numpy as jnp
from jax import lax

B = 256
K = 256
W = 40
NT = 20
N = 5120


def draw_tile_lists(key, part):
    key = jax.random.fold_in(key, 7)
    keys = jax.random.split(key, NT)
    offsets = jax.vmap(lambda single: jax.random.permutation(single, W))(keys)
    rows = jnp.arange(NT, dtype=jnp.int32)[:, None]
    return jnp.clip(rows + offsets.astype(jnp.int32) - W // 2, 0, NT - 1).astype(jnp.int32)


def draw_live_counts(key, part):
    key = jax.random.fold_in(key, 5)
    first, second, third = jax.random.split(key, 3)
    counts = jax.random.randint(first, (NT,), W // 4, W + 1)
    fullest = jax.random.randint(second, (), 0, NT)
    emptiest = (fullest + 1 + jax.random.randint(third, (), 0, max(NT - 1, 1))) % NT
    rows = jnp.arange(NT, dtype=jnp.int32)
    counts = jnp.where(rows == fullest, W, counts)
    counts = jnp.where(rows == emptiest, W // 4, counts)
    return counts.astype(jnp.int32)


def draw_residual(key, part):
    key = jax.random.fold_in(key, 11)
    first = jax.random.fold_in(key, 0)
    ramp = jnp.exp(math.log(3.0) * jnp.arange(N, dtype=jnp.float32) / N)[None, :]
    return jax.random.normal(first, (K, N), jnp.float32) * ramp


def plant(drawn, stream_key, smallest, largest):
    extent = drawn.shape
    place = [jax.random.randint(jax.random.fold_in(stream_key, axis), (), 0, extent[axis]) for axis in range(len(extent))]
    drawn = drawn.at[tuple(place)].set(smallest)
    longest = extent.index(max(extent))
    place[longest] = (place[longest] + 1) % extent[longest]
    return drawn.at[tuple(place)].set(largest)


def shard_levels(key, dims, cuts, smallest, high):
    factor_of = 1.0
    for position, blocks in cuts:
        steps = jax.random.uniform(jax.random.fold_in(jax.random.fold_in(key, 6), position), (blocks,), jnp.float32, smallest / len(cuts), high / len(cuts))
        factor_of = factor_of * jnp.repeat(jnp.exp(steps), dims[position] // blocks).reshape((-1,) + (1,) * (len(dims) - 1 - position))
    return factor_of


def bell_draw(rng, shape, scale, bound, pieces=(), held_as=jnp.bfloat16):
    drawn = jax.random.normal(rng, shape, jnp.float32) * scale
    if len(pieces) > 0:
        drawn = shard_levels(rng, shape, pieces, -0.22, 0.18) * drawn
    return jnp.clip(drawn, min=-bound, max=bound).astype(held_as)


def setup_inputs(seed: int = 0, part: int = 0) -> dict:
    key_list = jax.random.split(jax.random.key(seed), 8)
    part_splits = jax.random.split(jax.random.fold_in(key_list[7], part), 8)
    return {
        "ld_tiles": bell_draw(part_splits[0], (NT, W, B, B), (4 * W * B) ** -0.5, 0.03125, ((0, 4), (1, 4))),
        "tile_lists": draw_tile_lists(jax.random.fold_in(jax.random.fold_in(key_list[7], part), 71), part),
        "live_counts": draw_live_counts(jax.random.fold_in(jax.random.fold_in(key_list[7], part), 71), part),
        "typed_mask": plant((jax.random.randint(part_splits[3], (N,), 0, 4) < 3).astype(jnp.int32), jax.random.fold_in(part_splits[3], 1), 0, 1),
        "solution": bell_draw(part_splits[4], (K, N), 1.0, 6.0, ((0, 4), (1, 4)), jnp.float32),
        "residual": draw_residual(jax.random.fold_in(jax.random.fold_in(key_list[7], part), 71), part),
        "direction": bell_draw(part_splits[6], (K, N), 1.0, 6.0, ((0, 4), (1, 4)), jnp.float32),
    }


def window_product(vectors, ld_tiles, tile_lists, live_counts):
    traits = vectors.shape[0]
    tile_total = ld_tiles.shape[0]
    slots = ld_tiles.shape[1]
    tile_size = ld_tiles.shape[2]
    blocks = vectors.reshape(traits, tile_total, tile_size)

    def one_row(index):
        picked = jnp.take(blocks, tile_lists[index].astype(jnp.int32), axis=1).astype(jnp.float32)
        active = (jnp.arange(slots, dtype=jnp.int32) < live_counts[index]).astype(jnp.float32)
        picked = picked * active[None, :, None]
        return jnp.einsum('ksj,sij->ki', picked, ld_tiles[index].astype(jnp.float32))

    result = lax.map(one_row, jnp.arange(tile_total, dtype=jnp.int32))
    return jnp.transpose(result, (1, 0, 2)).reshape(traits, tile_total * tile_size)


def reference(ld_tiles, tile_lists, live_counts, typed_mask, solution, residual, direction):
    typed_rows = typed_mask.astype(jnp.float32)[None, :]
    masked = (direction * typed_rows).astype(jnp.bfloat16)
    spread = window_product(masked, ld_tiles, tile_lists, live_counts)
    image = typed_rows * direction + typed_rows * spread + 0.1 * direction
    before = jnp.sum(residual * residual, axis=1)
    curve = jnp.sum(direction * image, axis=1)
    alpha = (before / curve)[:, None]
    solution_next = solution + alpha * direction
    residual_next = residual - alpha * image
    after = jnp.sum(residual_next * residual_next, axis=1)
    direction_next = residual_next + (after / before)[:, None] * direction
    weights = (solution_next * typed_rows).astype(jnp.bfloat16)
    imputed = (1.0 - typed_rows) * window_product(weights, ld_tiles, tile_lists, live_counts)
    return (solution_next, residual_next, direction_next, imputed)
```

```python
import functools

import jax
import jax.numpy as jnp
from jax import lax
from jax.experimental import pallas as pl
from jax.experimental.pallas import tpu as pltpu
from jax.sharding import PartitionSpec as P

W = 40


def from_behind(block, axis, distance):
    devices = range(lax.axis_size(axis))
    route = [(i - distance, i) for i in devices if i - distance in devices]
    return lax.ppermute(block, axis, route)


def gather_window(block, extent):
    rows, cols = lax.axis_size("row"), lax.axis_size("col")
    if extent >= rows - 1:
        whole = lax.all_gather(block, ("row", "col"), axis=0, tiled=False)
        return whole.reshape((rows, cols) + block.shape)
    mine = lax.all_gather(block, "col", axis=0, tiled=False)
    pieces = [
        mine if offset == 0 else from_behind(mine, "row", -offset)
        for offset in range(-extent, extent + 1)
    ]
    return jnp.stack(pieces)


def product_kernel(tile_rows, slots, tile_size, place_ref, live_ref, v_ref, ld_ref, out_ref):
    t = pl.program_id(0)
    cols, depth = v_ref.shape[1], v_ref.shape[2]
    traits = cols * depth

    def one_slot(s, total):
        place = place_ref[t, s]
        piece = place // tile_rows
        start = pl.multiple_of((place - piece * tile_rows) * tile_size, tile_size)
        picked = v_ref[piece, :, :, pl.ds(start, tile_size)].reshape(traits, tile_size)
        return total + lax.dot_general(
            picked, ld_ref[0, s], (((1,), (1,)), ((), ())),
            preferred_element_type=jnp.float32,
        )

    total = lax.fori_loop(
        0, live_ref[t], one_slot, jnp.zeros((traits, tile_size), jnp.float32)
    )
    out_ref[...] = total.reshape(cols, depth, tile_size)


def window_product(vectors, ld_tiles, place, live):
    tile_rows, slots, tile_size, _ = ld_tiles.shape
    pieces, cols, depth, width = vectors.shape
    return pl.pallas_call(
        functools.partial(product_kernel, tile_rows, slots, tile_size),
        grid=(tile_rows,),
        in_specs=[
            pl.BlockSpec(memory_space=pltpu.SMEM),
            pl.BlockSpec(memory_space=pltpu.SMEM),
            pl.BlockSpec((pieces, cols, depth, width), lambda t: (0, 0, 0, 0)),
            pl.BlockSpec((1, slots, tile_size, tile_size), lambda t: (t, 0, 0, 0)),
        ],
        out_specs=pl.BlockSpec((cols, depth, tile_size), lambda t: (0, 0, t)),
        out_shape=jax.ShapeDtypeStruct((cols, depth, tile_rows * tile_size), jnp.float32),
        compiler_params=pltpu.CompilerParams(vmem_limit_bytes=40 * 1024 * 1024),
        cost_estimate=pl.CostEstimate(
            flops=2 * cols * depth * tile_rows * slots * tile_size**2,
            bytes_accessed=2 * ld_tiles.size + 2 * vectors.size + 4 * cols * depth * width,
            transcendentals=0,
        ),
        name="window_product",
    )(place, live, vectors, ld_tiles)


def local(ld_tiles, tile_lists, live_counts, typed_mask, solution, residual, direction):
    tile_rows, slots = tile_lists.shape
    extent = min((W // 2 + tile_rows - 1) // tile_rows, lax.axis_size("row") - 1)
    lowest = lax.axis_index("row") - extent
    if extent >= lax.axis_size("row") - 1:
        lowest = 0
    place = tile_lists - lowest * tile_rows
    live = jnp.clip(live_counts - lax.axis_index("col") * slots, 0, slots)

    typed = typed_mask.astype(jnp.float32)[None, :]
    masked = (direction * typed).astype(jnp.bfloat16)
    known = (solution * typed).astype(jnp.bfloat16)
    masked_all = gather_window(masked, extent)
    known_all = gather_window(known, extent)
    spread = lax.psum_scatter(
        window_product(masked_all, ld_tiles, place, live), "col", scatter_dimension=0
    )
    image = typed * direction + typed * spread + 0.1 * direction
    before, curve, cross, square = lax.psum(
        jnp.stack([
            jnp.sum(residual * residual, axis=1),
            jnp.sum(direction * image, axis=1),
            jnp.sum(residual * image, axis=1),
            jnp.sum(image * image, axis=1),
        ]),
        "row",
    )
    alpha = before / curve
    after = before + alpha * (alpha * square - 2.0 * cross)
    beta = after / before
    alpha, beta = alpha[:, None], beta[:, None]
    solution_next = solution + alpha * direction
    residual_next = residual - alpha * image
    direction_next = residual_next + beta * direction
    held = lax.psum_scatter(
        window_product(known_all, ld_tiles, place, live), "col", scatter_dimension=0
    )
    imputed = (1.0 - typed) * (held + alpha * spread)
    return (solution_next, residual_next, direction_next, imputed)


def solution(mesh):
    in_specs = (
        P(("seg", "row"), "col", None, None),
        P(("seg", "row"), "col"),
        P(("seg", "row")),
        P(("seg", "row")),
        P(("seg", "col"), "row"),
        P(("seg", "col"), "row"),
        P(("seg", "col"), "row"),
    )
    out_specs = (P(("seg", "col"), "row"),) * 4
    return jax.shard_map(local, mesh=mesh, in_specs=in_specs, out_specs=out_specs, check_vma=False)
```

```python
import functools

import jax
import jax.numpy as jnp
from jax import lax
from jax.experimental import pallas as pl
from jax.experimental.pallas import tpu as pltpu
from jax.sharding import PartitionSpec as P

W = 40


def shifted(block, axis, distance):
    size = lax.axis_size(axis)
    return lax.ppermute(block, axis, [(i, (i + distance) % size) for i in range(size)])


def swapped(block, axis, bit):
    size = lax.axis_size(axis)
    return lax.ppermute(block, axis, [(i, i ^ bit) for i in range(size)])


def row_offsets():
    return lax.axis_size("row")


def product_kernel(counts, place_ref, near_ref, far_ref, *refs):
    pieces, groups, depth, tile_size, slots = counts
    parts = refs[: pieces * groups]
    out_refs = refs[pieces * groups : pieces * groups + groups]
    held, sems = refs[pieces * groups + groups :]
    t = pl.program_id(0)
    traits = groups * depth

    @pl.when(t == 0)
    def _():
        copies = [
            pltpu.make_async_copy(
                parts[g * pieces + p], held.at[p, pl.ds(g * depth, depth)], sems.at[g * pieces + p]
            )
            for g in range(groups)
            for p in range(pieces)
        ]
        for copy in copies:
            copy.start()
        held[pieces, :, pl.ds(0, tile_size)] = jnp.zeros((traits, tile_size), held.dtype)
        for copy in copies:
            copy.wait()

    total = jnp.zeros((traits, tile_size), jnp.float32)
    for s in range(2 * slots):
        piece = place_ref[0, t, s]
        start = pl.multiple_of(place_ref[1, t, s], tile_size)
        picked = held[piece, :, pl.ds(start, tile_size)]
        tile = near_ref[0, s] if s < slots else far_ref[0, s - slots]
        total = total + lax.dot_general(
            picked, tile, (((1,), (1,)), ((), ())), preferred_element_type=jnp.float32
        )
    for g in range(groups):
        out_refs[g][...] = total[g * depth : (g + 1) * depth]


def window_product(groups, near, far, place):
    tile_rows, slots, tile_size, _ = near.shape
    pieces = len(groups[0])
    depth, width = groups[0][0].shape
    count = len(groups)
    counts = (pieces, count, depth, tile_size, slots)
    ld_spec = pl.BlockSpec((1, slots, tile_size, tile_size), lambda t: (t, 0, 0, 0))
    return pl.pallas_call(
        functools.partial(product_kernel, counts),
        grid=(tile_rows,),
        in_specs=[pl.BlockSpec(memory_space=pltpu.SMEM), ld_spec, ld_spec]
        + [pl.BlockSpec(memory_space=pl.ANY)] * (pieces * count),
        out_specs=[pl.BlockSpec((depth, tile_size), lambda t: (0, t))] * count,
        out_shape=[jax.ShapeDtypeStruct((depth, width), jnp.float32)] * count,
        scratch_shapes=[
            pltpu.VMEM((pieces + 1, count * depth, width), jnp.bfloat16),
            pltpu.SemaphoreType.DMA((pieces * count,)),
        ],
        compiler_params=pltpu.CompilerParams(vmem_limit_bytes=48 * 1024 * 1024),
        cost_estimate=pl.CostEstimate(
            flops=4 * count * depth * tile_rows * slots * tile_size**2,
            bytes_accessed=4 * near.size + (2 * pieces + 4) * count * depth * width,
            transcendentals=0,
        ),
        name="window_product",
    )(place, near, far, *[part for group in groups for part in group])


def local(ld_tiles, tile_lists, live_counts, typed_mask, solution, residual, direction):
    tile_rows, slots = tile_lists.shape
    tile_size = ld_tiles.shape[2]
    rows, cols = lax.axis_size("row"), lax.axis_size("col")
    bits = [1 << b for b in range(1, cols.bit_length() - 1)]
    reach = (W // 2 + tile_rows - 1) // tile_rows
    if 2 * reach + 1 >= rows:
        behind = list(range(rows))
    else:
        behind = list(range(reach + 1)) + list(range(rows - reach, rows))

    def along_row(block):
        return [block if d == 0 else shifted(block, "row", d) for d in behind]

    def along_col(parts):
        groups = [parts]
        for bit in bits:
            groups = groups + [[swapped(p, "col", bit) for p in g] for g in groups]
        return groups

    def summed(sums):
        for bit in reversed(bits):
            half = len(sums) // 2
            moved = [swapped(s, "col", bit) for s in sums[half:]]
            sums = [a + b for a, b in zip(sums[:half], moved)]
        return sums[0]

    typed = typed_mask.astype(jnp.float32)[None, :]
    masked = (direction * typed).astype(jnp.bfloat16)
    masked_parts = along_row(masked)
    far = swapped(ld_tiles, "col", 1)

    me = lax.axis_index("row")
    distance = lax.rem(me - tile_lists // tile_rows + rows, rows)
    piece = jnp.where(distance <= behind[len(behind) // 2], distance, distance - rows + len(behind))
    if len(behind) == rows:
        piece = distance
    slot = lax.axis_index("col") * slots + jnp.arange(slots, dtype=jnp.int32)
    live = slot[None, :] < live_counts[:, None]
    place = jnp.stack([
        jnp.where(live, piece, len(behind)),
        jnp.where(live, (tile_lists % tile_rows) * tile_size, 0),
    ])
    place = jnp.concatenate([place, swapped(place, "col", 1)], axis=2)

    masked_groups = along_col(masked_parts)
    known = (solution * typed).astype(jnp.bfloat16)
    known, *masked_parts = lax.optimization_barrier((known, *masked_parts))
    known_groups = along_col(along_row(known))

    spread = summed(window_product(masked_groups, ld_tiles, far, place))
    image = typed * direction + typed * spread + 0.1 * direction
    sums = jnp.stack([
        jnp.sum(residual * residual, axis=1),
        jnp.sum(direction * image, axis=1),
        jnp.sum(residual * image, axis=1),
        jnp.sum(image * image, axis=1),
    ])
    if rows <= 4:
        total = sums
        for d in range(1, rows):
            total = total + shifted(sums, "row", d)
    else:
        total = lax.psum(sums, "row")
    before, curve, cross, square = total
    alpha = before / curve
    after = before + alpha * (alpha * square - 2.0 * cross)
    beta = after / before
    alpha, beta = alpha[:, None], beta[:, None]
    solution_next = solution + alpha * direction
    residual_next = residual - alpha * image
    direction_next = residual_next + beta * direction
    held = summed(window_product(known_groups, ld_tiles, far, place))
    imputed = (1.0 - typed) * (held + alpha * spread)
    return (solution_next, residual_next, direction_next, imputed)


def solution(mesh):
    in_specs = (
        P(("seg", "row"), "col", None, None),
        P(("seg", "row"), "col"),
        P(("seg", "row")),
        P(("seg", "row")),
        P(("seg", "col"), "row"),
        P(("seg", "col"), "row"),
        P(("seg", "col"), "row"),
    )
    out_specs = (P(("seg", "col"), "row"),) * 4
    return jax.shard_map(local, mesh=mesh, in_specs=in_specs, out_specs=out_specs, check_vma=False)
```

```python
import functools

import jax
import jax.numpy as jnp
from jax import lax
from jax.experimental import pallas as pl
from jax.experimental.pallas import tpu as pltpu
from jax.sharding import PartitionSpec as P

W = 40


def shifted(block, axis, distance):
    size = lax.axis_size(axis)
    return lax.ppermute(block, axis, [(i, (i + distance) % size) for i in range(size)])


def swapped(block, axis, bit):
    size = lax.axis_size(axis)
    return lax.ppermute(block, axis, [(i, i ^ bit) for i in range(size)])


def product_kernel(counts, place_ref, near_ref, far_ref, *refs):
    pieces, groups, depth, tile_size, slots, tile_rows, flip = counts
    parts = refs[: pieces * groups]
    out_refs = refs[pieces * groups : pieces * groups + groups]
    held, turned, sems = refs[pieces * groups + groups :]
    t = pl.program_id(0)
    traits = groups * depth

    @pl.when(t == 0)
    def _():
        copies = [
            pltpu.make_async_copy(
                parts[g * pieces + p], held.at[p, pl.ds(g * depth, depth)], sems.at[g * pieces + p]
            )
            for g in range(groups)
            for p in range(pieces)
        ]
        for copy in copies:
            copy.start()
        held[pieces, :, pl.ds(0, tile_size)] = jnp.zeros((traits, tile_size), held.dtype)
        for copy in copies:
            copy.wait()
        if flip:
            for p in range(pieces):
                for r in range(tile_rows):
                    turned[p * tile_rows + r] = held[p, :, r * tile_size : (r + 1) * tile_size].T
            turned[pieces * tile_rows] = jnp.zeros((tile_size, traits), held.dtype)

    if flip:
        total = jnp.zeros((tile_size, traits), jnp.float32)
    else:
        total = jnp.zeros((traits, tile_size), jnp.float32)
    for s in range(2 * slots):
        tile = near_ref[0, s] if s < slots else far_ref[0, s - slots]
        if flip:
            picked = turned[place_ref[2, t, s]]
            total = total + jnp.dot(tile, picked, preferred_element_type=jnp.float32)
        else:
            start = pl.multiple_of(place_ref[1, t, s], tile_size)
            picked = held[place_ref[0, t, s], :, pl.ds(start, tile_size)]
            total = total + lax.dot_general(
                picked, tile, (((1,), (1,)), ((), ())), preferred_element_type=jnp.float32
            )
    if flip:
        total = total.T
    for g in range(groups):
        out_refs[g][...] = total[g * depth : (g + 1) * depth]


def window_product(groups, near, far, place, flip):
    tile_rows, slots, tile_size, _ = near.shape
    pieces = len(groups[0])
    depth, width = groups[0][0].shape
    count = len(groups)
    counts = (pieces, count, depth, tile_size, slots, tile_rows, flip)
    ld_spec = pl.BlockSpec((1, slots, tile_size, tile_size), lambda t: (t, 0, 0, 0))
    return pl.pallas_call(
        functools.partial(product_kernel, counts),
        grid=(tile_rows,),
        in_specs=[pl.BlockSpec(memory_space=pltpu.SMEM), ld_spec, ld_spec]
        + [pl.BlockSpec(memory_space=pl.ANY)] * (pieces * count),
        out_specs=[pl.BlockSpec((depth, tile_size), lambda t: (0, t))] * count,
        out_shape=[jax.ShapeDtypeStruct((depth, width), jnp.float32)] * count,
        scratch_shapes=[
            pltpu.VMEM((pieces + 1, count * depth, width), jnp.bfloat16),
            pltpu.VMEM((pieces * tile_rows + 1, tile_size, count * depth), jnp.bfloat16),
            pltpu.SemaphoreType.DMA((pieces * count,)),
        ],
        compiler_params=pltpu.CompilerParams(vmem_limit_bytes=24 * 1024 * 1024),
        cost_estimate=pl.CostEstimate(
            flops=4 * count * depth * tile_rows * slots * tile_size**2,
            bytes_accessed=4 * near.size + (2 * pieces + 4) * count * depth * width,
            transcendentals=0,
        ),
        name="window_product",
    )(place, near, far, *[part for group in groups for part in group])


def local(ld_tiles, tile_lists, live_counts, typed_mask, solution, residual, direction):
    tile_rows, slots = tile_lists.shape
    tile_size = ld_tiles.shape[2]
    rows, cols = lax.axis_size("row"), lax.axis_size("col")
    bits = [1 << b for b in range(1, cols.bit_length() - 1)]
    reach = (W // 2 + tile_rows - 1) // tile_rows
    if 2 * reach + 1 >= rows:
        behind = list(range(rows))
    else:
        behind = list(range(reach + 1)) + list(range(rows - reach, rows))

    def along_row(block):
        return [block if d == 0 else shifted(block, "row", d) for d in behind]

    def along_col(parts):
        groups = [parts]
        for bit in bits:
            groups = groups + [[swapped(p, "col", bit) for p in g] for g in groups]
        return groups

    def summed(sums):
        for bit in reversed(bits):
            half = len(sums) // 2
            moved = [swapped(s, "col", bit) for s in sums[half:]]
            sums = [a + b for a, b in zip(sums[:half], moved)]
        return sums[0]

    typed = typed_mask.astype(jnp.float32)[None, :]
    masked = (direction * typed).astype(jnp.bfloat16)
    known = (solution * typed).astype(jnp.bfloat16)
    masked, known = lax.optimization_barrier((masked, known))
    masked_parts = along_row(masked)
    far = swapped(ld_tiles, "col", 1)
    masked_groups = along_col(masked_parts)

    me = lax.axis_index("row")
    distance = lax.rem(me - tile_lists // tile_rows + rows, rows)
    piece = jnp.where(distance <= behind[len(behind) // 2], distance, distance - rows + len(behind))
    if len(behind) == rows:
        piece = distance
    slot = lax.axis_index("col") * slots + jnp.arange(slots, dtype=jnp.int32)
    live = slot[None, :] < live_counts[:, None]
    inner = tile_lists % tile_rows
    place = jnp.stack([
        jnp.where(live, piece, len(behind)),
        jnp.where(live, inner * tile_size, 0),
        jnp.where(live, piece * tile_rows + inner, len(behind) * tile_rows),
    ])
    place, _ = lax.optimization_barrier((place, masked_parts[1]))
    place = jnp.concatenate([place, swapped(place, "col", 1)], axis=2)

    known, *_ = lax.optimization_barrier((known, *masked_parts))
    known_groups = along_col(along_row(known))

    spread = summed(window_product(masked_groups, ld_tiles, far, place, False))
    image = typed * direction + typed * spread + 0.1 * direction
    sums = jnp.stack([
        jnp.sum(residual * residual, axis=1),
        jnp.sum(direction * image, axis=1),
        jnp.sum(residual * image, axis=1),
        jnp.sum(image * image, axis=1),
    ])
    if rows <= 4:
        total = sums
        for d in range(1, rows):
            total = total + shifted(sums, "row", d)
    else:
        total = lax.psum(sums, "row")
    before, curve, cross, square = total
    alpha = before / curve
    after = before + alpha * (alpha * square - 2.0 * cross)
    beta = after / before
    alpha, beta = alpha[:, None], beta[:, None]
    solution_next = solution + alpha * direction
    residual_next = residual - alpha * image
    direction_next = residual_next + beta * direction
    held = summed(window_product(known_groups, ld_tiles, far, place, True))
    imputed = (1.0 - typed) * (held + alpha * spread)
    return (solution_next, residual_next, direction_next, imputed)


def solution(mesh):
    in_specs = (
        P(("seg", "row"), "col", None, None),
        P(("seg", "row"), "col"),
        P(("seg", "row")),
        P(("seg", "row")),
        P(("seg", "col"), "row"),
        P(("seg", "col"), "row"),
        P(("seg", "col"), "row"),
    )
    out_specs = (P(("seg", "col"), "row"),) * 4
    return jax.shard_map(local, mesh=mesh, in_specs=in_specs, out_specs=out_specs, check_vma=False)
```
